128 devices in a mesh: space: 32 (over z, y_hi, x), mode: 4 (over y_lo, core).
Axes of the slice: x: 4, y: 4 (y_hi: 2, y_lo: 2; y = y_hi * 2 + y_lo), z: 4, core: 2. Of those that a mesh axis runs over, the one named last changes fastest.
Arguments:
- modes: bfloat16 [3, 512, 65536], P(None, 'mode', 'space'), may hold values from -6 to 6
- gradients: bfloat16 [3, 3, 512, 65536], P(None, None, 'mode', 'space'), may hold values from -6 to 6
- convecting_slab: bfloat16 [3, 16, 32768], P(None, None, 'space'), may hold values from -6 to 6
- connectivity: int32 [65536], P('space'), may hold values from 0 to 32767, as said below
- weights: float32 [65536], P('space'), may hold values from 0.25 to 4
Outputs:
- convection: float32 [512, 16, 512], P('space', None, 'mode')
The draws below stay inside these ranges and needn't reach their ends.
Inputs may be any that keep to these rules, and one draw needn't show every extreme that they name: Each node names a point of its own block: connectivity[q] // 1024 == q // 2048.
All inputs are finite; a program needn't handle non-finite values.
Results may differ from the reference program's by a relative error of at most 0.0041.
Values may be sent and summed in bfloat16 or wider, within the bound.
A program may use at most 128 MiB of HBM per device.

```python
import math
import jax
import jax.numpy as jnp
from jax import lax

M = 512
J = 16
QDEV = 2048
PDEV = 1024
NQ = 65536
NPTS = 32768


def draw_connectivity(key, part):
    key = jax.random.fold_in(key, 11)
    local = jax.random.randint(key, (NQ,), 0, PDEV)
    position = jnp.arange(NQ, dtype=jnp.int32)
    local = jnp.where(position % QDEV == QDEV - 1, PDEV - 1, local)
    return (position // QDEV * PDEV + local).astype(jnp.int32)


def levels(stream_key, extent, cuts, smallest, largest):
    gain, own = 1.0, jax.random.fold_in(stream_key, 6)
    for dim, blocks in cuts:
        heights = jnp.exp(jax.random.uniform(jax.random.fold_in(own, dim), (blocks,), jnp.float32, smallest / len(cuts), largest / len(cuts)))
        gain = gain * jnp.repeat(heights, extent[dim] // blocks).reshape([-1 if axis == dim else 1 for axis in range(len(extent))])
    return gain


def scatter_about(stream_key, dims, spread, most, cuts=(), held_as=jnp.bfloat16):
    entries = spread * jax.random.normal(stream_key, dims, jnp.float32)
    if cuts:
        entries = entries * levels(stream_key, dims, cuts, -0.22, 0.18)
    return jnp.clip(entries, -most, most).astype(held_as)


def setup_inputs(seed: int = 0) -> dict:
    splits = jax.random.split(jax.random.key(seed), 6)
    modes = scatter_about(splits[0], (3, M, NQ), 1.0, 6.0, ((1, 4), (2, 32)))
    gradients = scatter_about(splits[1], (3, 3, M, NQ), 1.0, 6.0, ((2, 4), (3, 32)))
    convecting_slab = scatter_about(splits[2], (3, J, NPTS), 1.0, 6.0, ((2, 32),))
    connectivity = draw_connectivity(jax.random.fold_in(splits[5], 71), 0)
    weights = jnp.clip(jnp.exp(math.log(4.0) - 2.7725887 * jax.random.uniform(splits[4], (NQ,), jnp.float32) ** levels(splits[4], (NQ,), ((0, 32),), -0.2, 0.2)), 0.25, 4.0)
    return {"modes": modes, "gradients": gradients, "convecting_slab": convecting_slab, "connectivity": connectivity, "weights": weights}


def advect_one(column, gradients):
    first = column[0].astype(jnp.float32)[None, None, :] * gradients[0].astype(jnp.float32)
    second = column[1].astype(jnp.float32)[None, None, :] * gradients[1].astype(jnp.float32)
    third = column[2].astype(jnp.float32)[None, None, :] * gradients[2].astype(jnp.float32)
    return (first + second + third).astype(jnp.bfloat16)


def reference(modes, gradients, convecting_slab, connectivity, weights):
    nodal = jnp.take(convecting_slab, connectivity, axis=2)
    weighted = (weights[None, None, :] * modes.astype(jnp.float32)).astype(jnp.bfloat16)

    def one_slab(column):
        advected = advect_one(column, gradients)
        return lax.dot_general(weighted, advected, (((0, 2), (0, 2)), ((), ())), preferred_element_type=jnp.float32)

    tensor = lax.map(one_slab, jnp.moveaxis(nodal, 1, 0))
    scale = (3.0 * NQ) ** -0.5
    return jnp.transpose(tensor, (1, 0, 2)) * scale
```

```python
import functools

import jax
import jax.numpy as jnp
from jax import lax
from jax.experimental import pallas as pl
from jax.experimental.pallas import tpu as pltpu
from jax.sharding import PartitionSpec as P

MESH = pl.DeviceIdType.MESH
F32 = jnp.float32
BF16 = jnp.bfloat16

Q = 2048
PTS = 1024
NB = 4
NT = 512
QH = 1024


def lanes(nt):
    return pl.ds(pl.multiple_of(nt * NT, NT), NT)


def kernel(
    scale,
    modes_hbm, grad_hbm, slab_hbm, conn_hbm, wts_hbm,
    out,
    mod, gr, slab, conn, wts, nod, we, wl, a, acc, sx, rx, sz, rz, hs, rh,
    ld, ys, yr, fs, fr, bs, br, xs, xr, zs, zr, hsem, hrem,
):
    s = lax.axis_index("space")
    m = lax.axis_index("mode")
    z, h, x, l, c = s // 8, (s // 4) % 2, s % 4, m // 2, m % 2

    def dev(z=z, h=h, x=x, l=l, c=c):
        return (z * 8 + h * 4 + x, l * 2 + c)

    def remote(src, dst, send, recv, to):
        return pltpu.make_async_remote_copy(src, dst, send, recv, device_id=to, device_id_type=MESH)

    def piece(ref, p, core):
        cr, e, q = p // 6, (p // 2) % 3, p % 2
        return ref.at[e, cr, :, core, :, pl.ds(q * QH, QH)]

    def ycopy(p):
        return remote(piece(we, p, c), piece(wl, p, c), ys.at[p], yr.at[p], dev(l=1 - l))

    def fcopy(p, core):
        return remote(piece(wl, p, core), piece(wl, p, core), fs.at[p], fr.at[p], dev(c=1 - c))

    def bcopy(e, core):
        return remote(we.at[e, :, :, core], we.at[e, :, :, core], bs.at[e], br.at[e], dev(c=1 - c))

    def xcopy(ci, nt, dx):
        to = (x + dx) % 4
        return remote(sx.at[ci, to, :, lanes(nt)], rx.at[ci, dx - 1, :, lanes(nt)],
                      xs.at[ci, dx - 1], xr.at[ci, nt, dx - 1], dev(x=to))

    def xcopy_all(ci, dx):
        to = (x + dx) % 4
        return remote(sx.at[ci, to], rx.at[ci, dx - 1], xs.at[ci, dx - 1], xr.at[ci, 0, dx - 1], dev(x=to))

    def zbase(ci):
        return 2 * l if ci < 2 else 2 * (1 - l)

    def zcopy(ci, nt, zi):
        to = zbase(ci) + zi
        slot = (to - z + 3) % 4
        return remote(sz.at[ci, zi, :, lanes(nt)], rz.at[ci, slot, :, lanes(nt)],
                      zs.at[ci, nt, zi], zr.at[ci, nt, slot], dev(z=to))

    def zrecv(ci, nt, slot):
        return remote(sz.at[ci, 0, :, lanes(nt)], rz.at[ci, slot, :, lanes(nt)],
                      zs.at[ci, nt, 0], zr.at[ci, nt, slot], dev(z=(z + 1) % 4))

    def hcopy(ci, nt):
        return remote(hs.at[ci, 1 - h, :, lanes(nt)], rh.at[ci, :, lanes(nt)],
                      hsem.at[ci, nt], hrem.at[ci, nt], dev(h=1 - h))

    def owns(ci):
        return z // 2 == (l if ci < 2 else 1 - l)

    loads = [
        pltpu.make_async_copy(wts_hbm, wts, ld.at[0]),
        pltpu.make_async_copy(modes_hbm.at[0], mod.at[0], ld.at[1]),
        pltpu.make_async_copy(modes_hbm.at[1], mod.at[1], ld.at[2]),
        pltpu.make_async_copy(modes_hbm.at[2], mod.at[2], ld.at[3]),
        pltpu.make_async_copy(conn_hbm, conn, ld.at[4]),
        pltpu.make_async_copy(slab_hbm, slab, ld.at[5]),
        pltpu.make_async_copy(grad_hbm, gr, ld.at[6]),
    ]
    barrier = pltpu.get_barrier_semaphore()
    peers = [dev(c=1 - c), dev(l=1 - l), dev(h=1 - h)]
    peers += [dev(x=(x + d) % 4) for d in (1, 2, 3)] + [dev(z=(z + d) % 4) for d in (1, 2, 3)]
    for load in loads:
        load.start()
    for to in peers:
        pl.semaphore_signal(barrier, 1, device_id=to, device_id_type=MESH)

    loads[0].wait()
    for e in range(3):
        loads[1 + e].wait()

        def weigh(t, _, e=e):
            ln = lanes(t)
            w = wts[:, ln]
            for xx in range(4):
                lo = (w * mod[e, xx * 16:xx * 16 + 16, ln].astype(F32))
                hi = (w * mod[e, 64 + xx * 16:64 + xx * 16 + 16, ln].astype(F32))
                for cr in range(2):
                    both = jnp.concatenate([lo[cr * 8:cr * 8 + 8], hi[cr * 8:cr * 8 + 8]], axis=0)
                    we[e, cr, xx, c, :, ln] = both.astype(BF16)
            return 0

        lax.fori_loop(0, NB, weigh, 0)
        if e == 0:
            pl.semaphore_wait(barrier, len(peers))
        ycopy(2 * e).start()
        ycopy(2 * e + 1).start()
    for p in range(6, 12):
        ycopy(p).start()
    for e in range(3):
        bcopy(e, c).start()

    loads[4].wait()
    loads[5].wait()

    def gather(t, _):
        ln = lanes(t)
        local = conn[:, ln] - s * PTS
        hot = (lax.broadcasted_iota(jnp.int32, (PTS, NT), 0) == local).astype(F32).astype(BF16)
        vals = jnp.dot(slab[...].reshape(48, PTS), hot, preferred_element_type=F32)
        nod[:, :, ln] = vals.reshape(3, 16, NT)
        return 0

    lax.fori_loop(0, NB, gather, 0)
    loads[6].wait()

    def advect(t, _):
        ln = lanes(t % 4)
        kk = pl.multiple_of((t // 4) * 16, 16)
        for e in range(3):
            g0, g1, g2 = (gr[d, e, pl.ds(kk, 16), ln].astype(F32) for d in range(3))
            for j in range(16):
                v = nod[0, j:j + 1, ln] * g0 + nod[1, j:j + 1, ln] * g1 + nod[2, j:j + 1, ln] * g2
                a[e, pl.ds(j * 128 + kk, 16), ln] = v.astype(BF16)
        return 0

    def forward(p):
        ycopy(p).wait_recv()
        fcopy(p, c).start()

    for sec in range(4):
        lax.fori_loop(sec * 8, sec * 8 + 8, advect, 0)
        forward(sec)

    for e in range(3):
        bcopy(e, 1 - c).wait_recv()

    def early(nt, _):
        rows = pl.ds(pl.multiple_of(nt * NT, NT), NT)
        tot = None
        for e in range(3):
            part = lax.dot_general(we[e].reshape(256, Q), a[e, rows, :], (((1,), (1,)), ((), ())),
                                   preferred_element_type=F32)
            tot = part if tot is None else tot + part
        sx[0:2, :, :, lanes(nt)] = tot.astype(BF16).reshape(2, 4, 32, NT)
        for ci in range(2):
            for dx in (1, 2, 3):
                xcopy(ci, nt, dx).start()
        return 0

    lax.fori_loop(0, 2, early, 0)
    forward(4)
    lax.fori_loop(2, 4, early, 0)
    forward(5)
    forward(6)

    def xsum(ci):
        def one(nt, _):
            ln = lanes(nt)
            for dx in (1, 2, 3):
                xcopy(ci, nt, dx).wait_recv()
            tot = sx[ci, x, :, ln].astype(F32)
            for i in range(3):
                tot = tot + rx[ci, i, :, ln].astype(F32)
            for zi in range(2):
                sz[ci, zi, :, ln] = tot[zi * 16:zi * 16 + 16].astype(BF16)

                @pl.when(zbase(ci) + zi != z)
                def _(zi=zi):
                    zcopy(ci, nt, zi).start()
            return 0

        lax.fori_loop(0, NB, one, 0)

    def zsum(ci):
        @pl.when(owns(ci))
        def _():
            def one(nt, _):
                ln = lanes(nt)
                for i in range(3):
                    zrecv(ci, nt, i).wait_recv()
                tot = sz[ci, z % 2, :, ln].astype(F32)
                for i in range(3):
                    tot = tot + rz[ci, i, :, ln].astype(F32)
                hs[ci, 0, :, ln] = tot[0:8]
                hs[ci, 1, :, ln] = tot[8:16]
                hcopy(ci, nt).start()
                return 0

            lax.fori_loop(0, NB, one, 0)

    def finish(ci):
        cr = ci % 2

        @pl.when(owns(ci))
        def _():
            def one(nt, _):
                ln = lanes(nt)
                hcopy(ci, nt).wait_recv()
                out[cr * 8:cr * 8 + 8, ln] = (hs[ci, h, :, ln] + rh[ci, :, ln]) * scale
                return 0

            lax.fori_loop(0, NB, one, 0)

    def late(cr, sl):
        p = cr * 6 + sl
        e, q = sl // 2, sl % 2
        fcopy(p, 1 - c).wait_recv()

        def one(nt, _):
            rows = pl.ds(pl.multiple_of(nt * NT, NT), NT)
            w = wl[e, cr, :, :, :, q * QH:(q + 1) * QH].reshape(128, QH)
            part = lax.dot_general(a[e, rows, q * QH:(q + 1) * QH], w, (((1,), (1,)), ((), ())),
                                   preferred_element_type=F32)
            if sl > 0:
                part = part + acc[rows, :]
            if sl < 5:
                acc[rows, :] = part
            else:
                ci = 2 + cr
                sx[ci, :, :, lanes(nt)] = part.T.astype(BF16).reshape(4, 32, NT)
                for dx in (1, 2, 3):
                    xcopy(ci, nt, dx).start()
            return 0

        lax.fori_loop(0, NB, one, 0)

    late(0, 0)
    late(0, 1)
    forward(7)
    late(0, 2)
    late(0, 3)
    forward(8)
    late(0, 4)
    late(0, 5)
    forward(9)
    late(1, 0)
    xsum(0)
    late(1, 1)
    xsum(1)
    late(1, 2)
    forward(10)
    zsum(0)
    late(1, 3)
    zsum(1)
    finish(0)
    finish(1)
    forward(11)
    late(1, 4)
    late(1, 5)
    xsum(2)
    zsum(2)
    xsum(3)
    finish(2)
    zsum(3)
    finish(3)

    for p in range(12):
        ycopy(p).wait_send()
        fcopy(p, c).wait_send()
    for e in range(3):
        bcopy(e, c).wait_send()
    for ci in range(4):
        for dx in (1, 2, 3):
            xcopy_all(ci, dx).wait_send()

        def drain(nt, _, ci=ci):
            for zi in range(2):
                @pl.when(zbase(ci) + zi != z)
                def _(zi=zi):
                    zcopy(ci, nt, zi).wait_send()

            @pl.when(owns(ci))
            def _():
                hcopy(ci, nt).wait_send()
            return 0

        lax.fori_loop(0, NB, drain, 0)


def on_device(modes, gradients, convecting_slab, connectivity, weights):
    nodes = modes.shape[2] * lax.axis_size("space")
    scale = (3.0 * nodes) ** (-0.5)
    dma, vmem = pltpu.SemaphoreType.DMA, pltpu.VMEM
    flat = pl.pallas_call(
        functools.partial(kernel, scale),
        name="convection",
        out_shape=jax.ShapeDtypeStruct((16, 2048), F32),
        in_specs=[pl.BlockSpec(memory_space=pl.ANY)] * 5,
        out_specs=pl.BlockSpec(memory_space=pltpu.VMEM),
        scratch_shapes=[
            vmem((3, 128, Q), BF16), vmem((3, 3, 128, Q), BF16), vmem((3, 16, PTS), BF16),
            vmem((1, Q), jnp.int32), vmem((1, Q), F32), vmem((3, 16, Q), F32),
            vmem((3, 2, 4, 2, 16, Q), BF16), vmem((3, 2, 4, 2, 16, Q), BF16),
            vmem((3, 2048, Q), BF16), vmem((2048, 128), F32),
            vmem((4, 4, 32, 2048), BF16), vmem((4, 3, 32, 2048), BF16),
            vmem((4, 2, 16, 2048), BF16), vmem((4, 3, 16, 2048), BF16),
            vmem((4, 2, 8, 2048), F32), vmem((4, 8, 2048), F32),
            dma((7,)), dma((12,)), dma((12,)), dma((12,)), dma((12,)), dma((3,)), dma((3,)),
            dma((4, 3)), dma((4, NB, 3)), dma((4, NB, 2)), dma((4, NB, 3)), dma((4, NB)), dma((4, NB)),
        ],
        compiler_params=pltpu.CompilerParams(
            collective_id=0, has_side_effects=True, vmem_limit_bytes=60 * 2**20),
        cost_estimate=pl.CostEstimate(flops=2 * 512 * 2048 * 6144, bytes_accessed=7 * 2**20, transcendentals=0),
    )(modes, gradients, convecting_slab, connectivity.reshape(1, Q), weights.reshape(1, Q))
    return flat.reshape(16, 16, 128)


def solution(mesh):
    return jax.shard_map(
        on_device,
        mesh=mesh,
        in_specs=(
            P(None, "mode", "space"),
            P(None, None, "mode", "space"),
            P(None, None, "space"),
            P("space"),
            P("space"),
        ),
        out_specs=P("space", None, "mode"),
        check_vma=False,
    )
```

```python
import functools

import jax
import jax.numpy as jnp
from jax import lax
from jax.experimental import pallas as pl
from jax.experimental.pallas import tpu as pltpu
from jax.sharding import PartitionSpec as P

MESH = pl.DeviceIdType.MESH
F32 = jnp.float32
BF16 = jnp.bfloat16

Q = 2048
QH = 1024
PTS = 1024
NB = 4
NT = 512
ZT = 768
JG = 8

WIDE, NARROW = 0, 1
BEGIN = (0, 192)
DEPTH = (96, 32)
TILES = (24, 8)


def lanes(nt, width=NT):
    if isinstance(nt, int):
        return pl.ds(nt * width, width)
    return pl.ds(pl.multiple_of(nt * width, width), width)


def first_four(shape):
    return lax.broadcasted_iota(jnp.int32, shape, 0) < 4


def kernel(
    scale,
    modes_hbm, grad_hbm, slab_hbm, conn_hbm, wts_hbm,
    out,
    mod, gr, slab, conn, wts, nod, we, wl, a0, a1, acc,
    sxw, rxw, sxn, rxn, sz, rz, hs, rh, sn, rn,
    ld, ys, yr, fs, fr, bs, br, xs, xr, zs, zr, hsem, hrem, ns, nr,
):
    s = lax.axis_index("space")
    m = lax.axis_index("mode")
    z, h, x, l, c = s // 8, (s // 4) % 2, s % 4, m // 2, m % 2
    halves = (a0, a1)
    sxs, rxs = (sxw, sxn), (rxw, rxn)

    def dev(z=z, h=h, x=x, l=l, c=c):
        return (z * 8 + h * 4 + x, l * 2 + c)

    def remote(src, dst, send, recv, to):
        return pltpu.make_async_remote_copy(src, dst, send, recv, device_id=to, device_id_type=MESH)

    def core_rows(ck, core):
        return pl.ds(pl.multiple_of(BEGIN[ck] + core * DEPTH[ck], 32), DEPTH[ck])

    def piece(ref, p, core):
        ck, e, q = p // 6, (p // 2) % 3, p % 2
        return ref.at[e, core_rows(ck, core), pl.ds(q * QH, QH)]

    def ycopy(p):
        return remote(piece(we, p, c), piece(wl, p, c), ys.at[p], yr.at[p], dev(l=1 - l))

    def fcopy(p, core):
        return remote(piece(wl, p, core), piece(wl, p, core), fs.at[p], fr.at[p], dev(c=1 - c))

    def bcopy(ck, core):
        part = we.at[:, core_rows(ck, core), :]
        return remote(part, part, bs.at[ck], br.at[ck], dev(c=1 - c))

    def xcopy(g, ck, nt, dx):
        to = (x + dx) % 4
        return remote(sxs[ck].at[g, to, :, lanes(nt)], rxs[ck].at[g, dx - 1, :, lanes(nt)],
                      xs.at[g, ck, dx - 1], xr.at[g, ck, nt, dx - 1], dev(x=to))

    def xcopy_all(g, ck, dx):
        to = (x + dx) % 4
        return remote(sxs[ck].at[g, to], rxs[ck].at[g, dx - 1],
                      xs.at[g, ck, dx - 1], xr.at[g, ck, 0, dx - 1], dev(x=to))

    def zbase(g):
        return 2 * l if g == 0 else 2 * (1 - l)

    def owns(g):
        return z // 2 == (l if g == 0 else 1 - l)

    def zcopy(g, nt, zi):
        to = zbase(g) + zi
        slot = (to - z + 3) % 4
        return remote(sz.at[g, zi, :, lanes(nt, ZT)], rz.at[g, slot, :, lanes(nt, ZT)],
                      zs.at[g, nt, zi], zr.at[g, nt, slot], dev(z=to))

    def zrecv(g, nt, slot):
        return remote(sz.at[g, 0, :, lanes(nt, ZT)], rz.at[g, slot, :, lanes(nt, ZT)],
                      zs.at[g, nt, 0], zr.at[g, nt, slot], dev(z=(z + 1) % 4))

    def hcopy(g, nt):
        return remote(hs.at[g, 1 - h, :, lanes(nt)], rh.at[g, :, lanes(nt)],
                      hsem.at[g, nt], hrem.at[g, nt], dev(h=1 - h))

    def ncopy(g, b, zi, hi):
        to = zbase(g) + zi
        slot = ((to - z + 4) % 4) * 2 + (hi - h + 2) % 2 - 1
        return remote(sn.at[g, zi, hi, :, lanes(b, 256)], rn.at[g, slot, :, lanes(b, 256)],
                      ns.at[g, b, zi, hi], nr.at[g, b, slot], dev(z=to, h=hi))

    def nrecv(g, b, slot):
        return remote(sn.at[g, 0, 0, :, lanes(b, 256)], rn.at[g, slot, :, lanes(b, 256)],
                      ns.at[g, b, 0, 0], nr.at[g, b, slot], dev(z=(z + 1) % 4))

    loads = [pltpu.make_async_copy(wts_hbm, wts, ld.at[0])]
    loads += [pltpu.make_async_copy(modes_hbm.at[e], mod.at[e], ld.at[1 + e]) for e in range(3)]
    loads += [pltpu.make_async_copy(conn_hbm, conn, ld.at[4]), pltpu.make_async_copy(slab_hbm, slab, ld.at[5])]
    loads += [pltpu.make_async_copy(grad_hbm.at[d], gr.at[d], ld.at[6 + d]) for d in range(3)]
    peers = [dev(c=1 - c), dev(l=1 - l)] + [dev(x=(x + d) % 4) for d in (1, 2, 3)]
    peers += [dev(z=(z + d) % 4, h=(h + k) % 2) for d in range(4) for k in range(2) if d + k > 0]
    for load in loads:
        load.start()
    barrier = pltpu.get_barrier_semaphore()
    for to in peers:
        pl.semaphore_signal(barrier, 1, device_id=to, device_id_type=MESH)

    loads[0].wait()
    for e in range(3):
        loads[1 + e].wait()

        def weigh(t, _, e=e):
            ln = lanes(t, 256)
            w = wts[:, ln]
            top = first_four((8, 256))
            wide, narrow = [], []
            for xx in range(4):
                lo = w * mod[e, xx * 16:xx * 16 + 16, ln].astype(F32)
                hi = w * mod[e, 64 + xx * 16:64 + xx * 16 + 16, ln].astype(F32)
                wide += [lo[:8], hi[:8], jnp.where(top, lo[8:], pltpu.roll(hi[8:], 4, 0))]
                narrow.append(jnp.where(top, pltpu.roll(lo[8:], 4, 0), hi[8:]))
            we[e, core_rows(WIDE, c), ln] = jnp.concatenate(wide, axis=0).astype(BF16)
            we[e, core_rows(NARROW, c), ln] = jnp.concatenate(narrow, axis=0).astype(BF16)
            return 0

        lax.fori_loop(0, Q // 256, weigh, 0)
        if e == 0:
            pl.semaphore_wait(barrier, len(peers))
        ycopy(2 * e).start()
        ycopy(2 * e + 1).start()
    for p in range(6, 12):
        ycopy(p).start()
    for ck in range(2):
        bcopy(ck, c).start()

    loads[4].wait()
    loads[5].wait()

    def gather(t, _):
        ln = lanes(t)
        local = conn[:, ln] - s * PTS
        hot = (lax.broadcasted_iota(jnp.int32, (PTS, NT), 0) == local).astype(F32).astype(BF16)
        vals = jnp.dot(slab[...].reshape(48, PTS), hot, preferred_element_type=F32)
        nod[:, :, ln] = vals.reshape(3, 16, NT)
        return 0

    lax.fori_loop(0, NB, gather, 0)
    for d in range(3):
        loads[6 + d].wait()

    def forward(p):
        ycopy(p).wait_recv()
        fcopy(p, c).start()

    def spread(g, ck, nt, tot):
        for xx in range(4):
            both = [tot[k * DEPTH[ck] + xx * TILES[ck]:k * DEPTH[ck] + (xx + 1) * TILES[ck]] for k in range(2)]
            sxs[ck][g, xx, :, lanes(nt)] = jnp.concatenate(both, axis=0).astype(BF16)
        for dx in (1, 2, 3):
            xcopy(g, ck, nt, dx).start()

    def advect(group):
        def some(t, _):
            row = pl.multiple_of((t // 2) * 16, 16)
            at = lanes(t % 2)
            for half in range(2):
                ln = pl.ds(pl.multiple_of(half * QH + (t % 2) * NT, NT), NT)
                for e in range(3):
                    g0, g1, g2 = (gr[d, e, pl.ds(row, 16), ln].astype(F32) for d in range(3))
                    for jj in range(JG):
                        j = group * JG + jj
                        v = nod[0, j:j + 1, ln] * g0 + nod[1, j:j + 1, ln] * g1 + nod[2, j:j + 1, ln] * g2
                        halves[half][e, pl.ds(j * 128 + row, 16), at] = v.astype(BF16)
            return 0

        lax.fori_loop(0, 16, some, 0)

    def early(nt):
        tot = None
        for e in range(3):
            for q in range(2):
                part = lax.dot_general(we[e, :, q * QH:(q + 1) * QH], halves[q][e, nt * NT:(nt + 1) * NT, :],
                                       (((1,), (1,)), ((), ())), preferred_element_type=F32)
                tot = part if tot is None else tot + part
        for ck in range(2):
            spread(0, ck, nt, tot[BEGIN[ck]:BEGIN[ck] + 2 * DEPTH[ck]])

    def late(p):
        ck, e, q = p // 6, (p // 2) % 3, p % 2
        rows = 2 * DEPTH[ck]
        fcopy(p, 1 - c).wait_recv()
        w = wl[e, BEGIN[ck]:BEGIN[ck] + rows, q * QH:(q + 1) * QH]
        for nt in range(NB):
            cols = slice(nt * NT, (nt + 1) * NT)
            part = lax.dot_general(halves[q][e, cols, :], w, (((1,), (1,)), ((), ())), preferred_element_type=F32)
            if p % 6 > 0:
                part = part + acc[cols, 0:rows]
            if p % 6 < 5:
                acc[cols, 0:rows] = part
            else:
                spread(1, ck, nt, part.T)

    def xsum(g, begin=0, end=NB):
        def one(nt, _):
            for dx in (1, 2, 3):
                xcopy(g, WIDE, nt, dx).wait_recv()
            tot = sxw[g, x, :, lanes(nt)].astype(F32)
            for i in range(3):
                tot = tot + rxw[g, i, :, lanes(nt)].astype(F32)
            for zi in range(2):
                own = tot[zi * 24:zi * 24 + 24]
                fold = jnp.concatenate([own[16:, :256], own[16:, 256:]], axis=0)
                sz[g, zi, :, lanes(nt, ZT)] = jnp.concatenate([own[:16], fold], axis=1).astype(BF16)

                @pl.when(zbase(g) + zi != z)
                def _(zi=zi):
                    zcopy(g, nt, zi).start()
            return 0

        lax.fori_loop(begin, end, one, 0)

    def zsum(g):
        @pl.when(owns(g))
        def _():
            def one(nt, _):
                for i in range(3):
                    zrecv(g, nt, i).wait_recv()
                tot = sz[g, z % 2, :, lanes(nt, ZT)].astype(F32)
                for i in range(3):
                    tot = tot + rz[g, i, :, lanes(nt, ZT)].astype(F32)
                mixed = jnp.concatenate([tot[:8, NT:], tot[8:, NT:]], axis=1)
                for hi in range(2):
                    hs[g, hi, :, lanes(nt)] = jnp.concatenate([tot[hi * 8:hi * 8 + 8, :NT], mixed], axis=0)
                hcopy(g, nt).start()
                return 0

            lax.fori_loop(0, NB, one, 0)

    def finish(g):
        @pl.when(owns(g))
        def _():
            def one(nt, _):
                hcopy(g, nt).wait_recv()
                tot = (hs[g, h, :, lanes(nt)] + rh[g, :, lanes(nt)]) * scale
                out[0:8, lanes(nt)] = tot[:8]
                upper = jnp.where(h == 0, tot[8:], pltpu.roll(tot[8:], 4, 0))
                out[8:12, lanes(nt)] = upper[:4]
                return 0

            lax.fori_loop(0, NB, one, 0)

    def xsum_narrow(g):
        for b in range(2):
            halved = [[], []]
            for nt in (2 * b, 2 * b + 1):
                for dx in (1, 2, 3):
                    xcopy(g, NARROW, nt, dx).wait_recv()
                tot = sxn[g, x, :, lanes(nt)].astype(F32)
                for i in range(3):
                    tot = tot + rxn[g, i, :, lanes(nt)].astype(F32)
                for zi in range(2):
                    halved[zi].append(tot[zi * 8:zi * 8 + 8])
            top = first_four((8, NT))
            for zi in range(2):
                left, right = halved[zi]
                for hi in range(2):
                    if hi == 0:
                        both = jnp.where(top, left, pltpu.roll(right, 4, 0))
                    else:
                        both = jnp.where(top, pltpu.roll(left, 4, 0), right)
                    fold = jnp.concatenate([both[:, :256], both[:, 256:]], axis=0)
                    sn[g, zi, hi, :, lanes(b, 256)] = fold.astype(BF16)

                    @pl.when(jnp.logical_or(zbase(g) + zi != z, h != hi))
                    def _(zi=zi, hi=hi, b=b):
                        ncopy(g, b, zi, hi).start()

    def finish_narrow(g):
        @pl.when(owns(g))
        def _():
            for b in range(2):
                for i in range(7):
                    nrecv(g, b, i).wait_recv()
                tot = sn[g, z % 2, h, :, lanes(b, 256)].astype(F32)
                for i in range(7):
                    tot = tot + rn[g, i, :, lanes(b, 256)].astype(F32)
                both = jnp.concatenate([tot[:8], tot[8:]], axis=1) * scale
                out[12:16, lanes(2 * b)] = both[:4]
                out[12:16, lanes(2 * b + 1)] = both[4:]

    advect(0)
    forward(0)
    for ck in range(2):
        bcopy(ck, 1 - c).wait_recv()
    early(0)
    forward(1)
    early(1)
    advect(1)
    forward(2)
    early(2)
    forward(3)
    early(3)
    late(0)
    late(1)
    late(2)
    forward(4)
    late(3)
    late(4)
    forward(5)
    late(5)
    forward(6)
    xsum(0)
    forward(7)
    late(6)
    forward(8)
    late(7)
    forward(9)
    xsum_narrow(0)
    late(8)
    forward(10)
    late(9)
    forward(11)
    late(10)
    xsum(1, 0, 1)
    late(11)
    xsum(1, 1, 4)
    zsum(0)
    finish_narrow(0)
    xsum_narrow(1)
    zsum(1)
    finish(0)
    finish_narrow(1)
    finish(1)

    for p in range(12):
        ycopy(p).wait_send()
        fcopy(p, c).wait_send()
    for ck in range(2):
        bcopy(ck, c).wait_send()
    for g in range(2):
        for ck in range(2):
            for dx in (1, 2, 3):
                xcopy_all(g, ck, dx).wait_send()

        for zi in range(2):
            @pl.when(zbase(g) + zi != z)
            def _(g=g, zi=zi):
                for nt in range(NB):
                    zcopy(g, nt, zi).wait_send()

            for hi in range(2):
                @pl.when(jnp.logical_or(zbase(g) + zi != z, h != hi))
                def _(g=g, zi=zi, hi=hi):
                    for b in range(2):
                        ncopy(g, b, zi, hi).wait_send()

        @pl.when(owns(g))
        def _(g=g):
            for nt in range(NB):
                hcopy(g, nt).wait_send()


def on_device(modes, gradients, convecting_slab, connectivity, weights):
    nodes = modes.shape[2] * lax.axis_size("space")
    scale = (3.0 * nodes) ** (-0.5)
    dma, vmem = pltpu.SemaphoreType.DMA, pltpu.VMEM
    flat = pl.pallas_call(
        functools.partial(kernel, scale),
        name="convection",
        out_shape=jax.ShapeDtypeStruct((16, 2048), F32),
        in_specs=[pl.BlockSpec(memory_space=pl.ANY)] * 5,
        out_specs=pl.BlockSpec(memory_space=pltpu.VMEM),
        scratch_shapes=[
            vmem((3, 128, Q), BF16), vmem((3, 3, 128, Q), BF16), vmem((3, 16, PTS), BF16),
            vmem((1, Q), jnp.int32), vmem((1, Q), F32), vmem((3, 16, Q), F32),
            vmem((3, 256, Q), BF16), vmem((3, 256, Q), BF16),
            vmem((3, 2048, QH), BF16), vmem((3, 2048, QH), BF16), vmem((2048, 192), F32),
            vmem((2, 4, 48, 2048), BF16), vmem((2, 3, 48, 2048), BF16),
            vmem((2, 4, 16, 2048), BF16), vmem((2, 3, 16, 2048), BF16),
            vmem((2, 2, 16, NB * ZT), BF16), vmem((2, 3, 16, NB * ZT), BF16),
            vmem((2, 2, 16, 2048), F32), vmem((2, 16, 2048), F32),
            vmem((2, 2, 2, 16, 512), BF16), vmem((2, 7, 16, 512), BF16),
            dma((9,)), dma((12,)), dma((12,)), dma((12,)), dma((12,)), dma((2,)), dma((2,)),
            dma((2, 2, 3)), dma((2, 2, NB, 3)), dma((2, NB, 2)), dma((2, NB, 3)), dma((2, NB)), dma((2, NB)),
            dma((2, 2, 2, 2)), dma((2, 2, 7)),
        ],
        compiler_params=pltpu.CompilerParams(
            collective_id=0, has_side_effects=True, vmem_limit_bytes=60 * 2**20),
        cost_estimate=pl.CostEstimate(flops=2 * 512 * 2048 * 6144, bytes_accessed=7 * 2**20, transcendentals=0),
    )(modes, gradients, convecting_slab, connectivity.reshape(1, Q), weights.reshape(1, Q))
    return flat.reshape(16, 16, 128)


def solution(mesh):
    return jax.shard_map(
        on_device,
        mesh=mesh,
        in_specs=(
            P(None, "mode", "space"),
            P(None, None, "mode", "space"),
            P(None, None, "space"),
            P("space"),
            P("space"),
        ),
        out_specs=P("space", None, "mode"),
        check_vma=False,
    )
```

```python
import functools

import jax
import jax.numpy as jnp
from jax import lax
from jax.experimental import pallas as pl
from jax.experimental.pallas import tpu as pltpu
from jax.sharding import PartitionSpec as P

MESH = pl.DeviceIdType.MESH
F32 = jnp.float32
BF16 = jnp.bfloat16

Q = 2048
QH = 1024
PTS = 1024
NB = 4
NT = 512
ZT = 768
JG = 8

WIDE, NARROW = 0, 1
BEGIN = (0, 192)
DEPTH = (96, 32)
TILES = (24, 8)


PARTS = {ck: [(ck, e, q * QH, QH) for e in range(3) for q in range(2)] for ck in (WIDE, NARROW)}
for part in PARTS.values():
    part[-1:] = [part[-1][:3] + (QH // 2,), part[-1][:2] + (QH + QH // 2, QH // 2)]
PIECES = [PARTS[WIDE][0], PARTS[NARROW][0]] + PARTS[WIDE][1:] + PARTS[NARROW][1:]
NP = len(PIECES)
LAST = (7, 13)


def lanes(nt, width=NT):
    if isinstance(nt, int):
        return pl.ds(nt * width, width)
    return pl.ds(pl.multiple_of(nt * width, width), width)


def first_four(shape):
    return lax.broadcasted_iota(jnp.int32, shape, 0) < 4


def kernel(
    scale,
    modes_hbm, grad_hbm, slab_hbm, conn_hbm, wts_hbm,
    out,
    mod, gr, slab, conn, wts, nod, we, wl, a0, a1, accw, accn,
    sxw, rxw, sxn, rxn, sz, rz, hs, rh, sn, rn, res,
    os, ld, ys, yr, fs, fr, bs, br, xs, xr, zs, zr, hsem, hrem, ns, nr,
):
    s = lax.axis_index("space")
    m = lax.axis_index("mode")
    z, h, x, l, c = s // 8, (s // 4) % 2, s % 4, m // 2, m % 2
    halves = (a0, a1)
    sxs, rxs = (sxw, sxn), (rxw, rxn)

    def dev(z=z, h=h, x=x, l=l, c=c):
        return (z * 8 + h * 4 + x, l * 2 + c)

    def remote(src, dst, send, recv, to):
        return pltpu.make_async_remote_copy(src, dst, send, recv, device_id=to, device_id_type=MESH)

    def core_rows(ck, core):
        return pl.ds(pl.multiple_of(BEGIN[ck] + core * DEPTH[ck], 32), DEPTH[ck])

    def piece(ref, p, core):
        ck, e, at, nodes = PIECES[p]
        return ref.at[e, core_rows(ck, core), pl.ds(at, nodes)]

    def ycopy(p):
        return remote(piece(we, p, c), piece(wl, p, c), ys.at[p], yr.at[p], dev(l=1 - l))

    def fcopy(p, core):
        return remote(piece(wl, p, core), piece(wl, p, core), fs.at[p], fr.at[p], dev(c=1 - c))

    def bcopy(ck, core):
        part = we.at[:, core_rows(ck, core), :]
        return remote(part, part, bs.at[ck], br.at[ck], dev(c=1 - c))

    def xcopy(g, ck, nt, dx):
        to = (x + dx) % 4
        return remote(sxs[ck].at[g, to, :, lanes(nt)], rxs[ck].at[g, dx - 1, :, lanes(nt)],
                      xs.at[g, ck, dx - 1], xr.at[g, ck, nt, dx - 1], dev(x=to))

    def xcopy_all(g, ck, dx):
        to = (x + dx) % 4
        return remote(sxs[ck].at[g, to], rxs[ck].at[g, dx - 1],
                      xs.at[g, ck, dx - 1], xr.at[g, ck, 0, dx - 1], dev(x=to))

    def zbase(g):
        return 2 * l if g == 0 else 2 * (1 - l)

    def owns(g):
        return z // 2 == (l if g == 0 else 1 - l)

    def zcopy(g, nt, zi):
        to = zbase(g) + zi
        slot = (to - z + 3) % 4
        return remote(sz.at[g, zi, :, lanes(nt, ZT)], rz.at[g, slot, :, lanes(nt, ZT)],
                      zs.at[g, nt, zi], zr.at[g, nt, slot], dev(z=to))

    def zrecv(g, nt, slot):
        return remote(sz.at[g, 0, :, lanes(nt, ZT)], rz.at[g, slot, :, lanes(nt, ZT)],
                      zs.at[g, nt, 0], zr.at[g, nt, slot], dev(z=(z + 1) % 4))

    def hcopy(g, nt):
        return remote(hs.at[g, 1 - h, :, lanes(nt)], rh.at[g, :, lanes(nt)],
                      hsem.at[g, nt], hrem.at[g, nt], dev(h=1 - h))

    def ncopy(g, b, zi, hi):
        to = zbase(g) + zi
        slot = ((to - z + 4) % 4) * 2 + (hi - h + 2) % 2 - 1
        return remote(sn.at[g, zi, hi, :, lanes(b, 256)], rn.at[g, slot, :, lanes(b, 256)],
                      ns.at[g, b, zi, hi], nr.at[g, b, slot], dev(z=to, h=hi))

    def nrecv(g, b, slot):
        return remote(sn.at[g, 0, 0, :, lanes(b, 256)], rn.at[g, slot, :, lanes(b, 256)],
                      ns.at[g, b, 0, 0], nr.at[g, b, slot], dev(z=(z + 1) % 4))

    loads = [pltpu.make_async_copy(wts_hbm, wts, ld.at[0])]
    for e in range(3):
        for q in range(2):
            part = (e, slice(None), pl.ds(q * QH, QH))
            loads.append(pltpu.make_async_copy(modes_hbm.at[part], mod.at[part], ld.at[1 + 2 * e + q]))
    loads += [pltpu.make_async_copy(conn_hbm, conn, ld.at[7]), pltpu.make_async_copy(slab_hbm, slab, ld.at[8])]
    for k in range(4):
        part = (slice(None), slice(None), pl.ds(32 * k, 32))
        loads.append(pltpu.make_async_copy(grad_hbm.at[part], gr.at[part], ld.at[9 + k]))
    peers = [dev(c=1 - c), dev(l=1 - l)] + [dev(x=(x + d) % 4) for d in (1, 2, 3)]
    peers += [dev(z=(z + d) % 4, h=(h + k) % 2) for d in range(4) for k in range(2) if d + k > 0]
    for load in loads:
        load.start()
    barrier = pltpu.get_barrier_semaphore()
    for to in peers:
        pl.semaphore_signal(barrier, 1, device_id=to, device_id_type=MESH)

    loads[0].wait()
    for e in range(3):
        def weigh(t, _, e=e):
            ln = lanes(t, 256)
            w = wts[:, ln]
            top = first_four((8, 256))
            wide, narrow = [], []
            for xx in range(4):
                lo = w * mod[e, xx * 16:xx * 16 + 16, ln].astype(F32)
                hi = w * mod[e, 64 + xx * 16:64 + xx * 16 + 16, ln].astype(F32)
                wide += [lo[:8], hi[:8], jnp.where(top, lo[8:], pltpu.roll(hi[8:], 4, 0))]
                narrow.append(jnp.where(top, pltpu.roll(lo[8:], 4, 0), hi[8:]))
            we[e, core_rows(WIDE, c), ln] = jnp.concatenate(wide, axis=0).astype(BF16)
            we[e, core_rows(NARROW, c), ln] = jnp.concatenate(narrow, axis=0).astype(BF16)
            return 0

        for q in range(2):
            loads[1 + 2 * e + q].wait()
            lax.fori_loop(4 * q, 4 * q + 4, weigh, 0)
            if e + q == 0:
                pl.semaphore_wait(barrier, len(peers))
            if e + q == 0:
                ycopy(0).start()
            ycopy(1 + 2 * e + q).start()
    for p in range(7, NP):
        ycopy(p).start()
    for ck in range(2):
        bcopy(ck, c).start()

    loads[7].wait()
    loads[8].wait()

    def gather(t, _):
        ln = lanes(t)
        local = conn[:, ln] - s * PTS
        hot = (lax.broadcasted_iota(jnp.int32, (128, NT), 0) == local % 128).astype(F32).astype(BF16)
        group = local // 128
        vals = jnp.zeros((48, NT), F32)
        for k in range(PTS // 128):
            one = jnp.dot(slab[:, :, k * 128:(k + 1) * 128].reshape(48, 128), hot, preferred_element_type=F32)
            vals = jnp.where(group == k, one, vals)
        nod[:, :, ln] = vals.reshape(3, 16, NT)
        return 0

    lax.fori_loop(0, NB, gather, 0)

    def forward(p):
        ycopy(p).wait_recv()
        fcopy(p, c).start()

    def spread(g, ck, nt, tot):
        for xx in range(4):
            both = [tot[k * DEPTH[ck] + xx * TILES[ck]:k * DEPTH[ck] + (xx + 1) * TILES[ck]] for k in range(2)]
            sxs[ck][g, xx, :, lanes(nt)] = jnp.concatenate(both, axis=0).astype(BF16)
        for dx in (1, 2, 3):
            xcopy(g, ck, nt, dx).start()

    def advect(group):
        def some(t, _):
            row = pl.multiple_of((t // 2) * 16, 16)
            at = lanes(t % 2)
            for half in range(2):
                ln = pl.ds(pl.multiple_of(half * QH + (t % 2) * NT, NT), NT)
                for e in range(3):
                    g0, g1, g2 = (gr[d, e, pl.ds(row, 16), ln].astype(F32) for d in range(3))
                    for jj in range(JG):
                        j = group * JG + jj
                        v = nod[0, j:j + 1, ln] * g0 + nod[1, j:j + 1, ln] * g1 + nod[2, j:j + 1, ln] * g2
                        halves[half][e, pl.ds(j * 128 + row, 16), at] = v.astype(BF16)
            return 0

        for k in range(4):
            if group == 0:
                loads[9 + k].wait()
            lax.fori_loop(4 * k, 4 * k + 4, some, 0)

    def early(nt):
        tot = None
        for e in range(3):
            for q in range(2):
                part = lax.dot_general(we[e, :, q * QH:(q + 1) * QH], halves[q][e, nt * NT:(nt + 1) * NT, :],
                                       (((1,), (1,)), ((), ())), preferred_element_type=F32)
                tot = part if tot is None else tot + part
        for ck in range(2):
            spread(0, ck, nt, tot[BEGIN[ck]:BEGIN[ck] + 2 * DEPTH[ck]])

    def product(p, nt, begin, end):
        _, e, at, nodes = PIECES[p]
        a = halves[at // QH][e, nt * NT:(nt + 1) * NT, at % QH:at % QH + nodes]
        return lax.dot_general(a, wl[e, begin:end, at:at + nodes], (((1,), (1,)), ((), ())), preferred_element_type=F32)

    def late_first():
        for p in range(2):
            fcopy(p, 1 - c).wait_recv()
        for nt in range(NB):
            cols = slice(nt * NT, (nt + 1) * NT)
            part = product(0, nt, 0, 256)
            accw[cols, :] = part[:, :192]
            accn[cols, :] = part[:, 128:]

    def late(*ps, then={}):
        ck = PIECES[ps[0]][0]
        for p in ps:
            fcopy(p, 1 - c).wait_recv()
        for nt in range(NB):
            cols = slice(nt * NT, (nt + 1) * NT)
            total = (accw, accn)[ck]
            begin, end = ((0, 192), (128, 256))[ck]
            part = total[cols, :]
            for p in ps:
                part = part + product(p, nt, begin, end)
            if ps[-1] < LAST[ck]:
                total[cols, :] = part
            else:
                rows = part.T
                spread(1, ck, nt, rows if ck == WIDE else rows[64:])
            if nt in then:
                forward(then[nt])

    def xsum(g, begin=0, end=NB):
        def one(nt, _):
            for dx in (1, 2, 3):
                xcopy(g, WIDE, nt, dx).wait_recv()
            tot = sxw[g, x, :, lanes(nt)].astype(F32)
            for i in range(3):
                tot = tot + rxw[g, i, :, lanes(nt)].astype(F32)
            for zi in range(2):
                own = tot[zi * 24:zi * 24 + 24]
                fold = jnp.concatenate([own[16:, :256], own[16:, 256:]], axis=0)
                sz[g, zi, :, lanes(nt, ZT)] = jnp.concatenate([own[:16], fold], axis=1).astype(BF16)

                @pl.when(zbase(g) + zi != z)
                def _(zi=zi):
                    zcopy(g, nt, zi).start()
            return 0

        lax.fori_loop(begin, end, one, 0)

    def zsum(g):
        @pl.when(owns(g))
        def _():
            def one(nt, _):
                for i in range(3):
                    zrecv(g, nt, i).wait_recv()
                tot = sz[g, z % 2, :, lanes(nt, ZT)].astype(F32)
                for i in range(3):
                    tot = tot + rz[g, i, :, lanes(nt, ZT)].astype(F32)
                mixed = jnp.concatenate([tot[:8, NT:], tot[8:, NT:]], axis=1)
                for hi in range(2):
                    pair = jnp.concatenate([tot[hi * 8:hi * 8 + 8, :NT], mixed], axis=0)
                    hs[g, hi, :, lanes(nt)] = pair
                hcopy(g, nt).start()
                return 0

            lax.fori_loop(0, NB, one, 0)

    def place(row, nt, part):
        for jj in range(4):
            res[row:row + part.shape[0], 4 * nt + jj, :] = part[:, jj * 128:(jj + 1) * 128]

    def store(row, rows, k):
        return pltpu.make_async_copy(res.at[pl.ds(row, rows)], out.at[pl.ds(row, rows)], os.at[k])

    def finish(g):
        @pl.when(owns(g))
        def _():
            for nt in range(NB):
                hcopy(g, nt).wait_recv()
                tot = (hs[g, h, :, lanes(nt)].astype(F32) + rh[g, :, lanes(nt)].astype(F32)) * scale
                place(0, nt, tot[:8])
                upper = jnp.where(h == 0, tot[8:], pltpu.roll(tot[8:], 4, 0))
                place(8, nt, upper[:4])
            store(0, 12, 0).start()

    def xsum_narrow(g):
        for b in range(2):
            halved = [[], []]
            for nt in (2 * b, 2 * b + 1):
                for dx in (1, 2, 3):
                    xcopy(g, NARROW, nt, dx).wait_recv()
                tot = sxn[g, x, :, lanes(nt)].astype(F32)
                for i in range(3):
                    tot = tot + rxn[g, i, :, lanes(nt)].astype(F32)
                for zi in range(2):
                    halved[zi].append(tot[zi * 8:zi * 8 + 8])
            top = first_four((8, NT))
            for zi in range(2):
                left, right = halved[zi]
                for hi in range(2):
                    if hi == 0:
                        both = jnp.where(top, left, pltpu.roll(right, 4, 0))
                    else:
                        both = jnp.where(top, pltpu.roll(left, 4, 0), right)
                    fold = jnp.concatenate([both[:, :256], both[:, 256:]], axis=0)
                    sn[g, zi, hi, :, lanes(b, 256)] = fold.astype(BF16)

                    @pl.when(jnp.logical_or(zbase(g) + zi != z, h != hi))
                    def _(zi=zi, hi=hi, b=b):
                        ncopy(g, b, zi, hi).start()

    def finish_narrow(g):
        @pl.when(owns(g))
        def _():
            for b in range(2):
                for i in range(7):
                    nrecv(g, b, i).wait_recv()
                tot = sn[g, z % 2, h, :, lanes(b, 256)].astype(F32)
                for i in range(7):
                    tot = tot + rn[g, i, :, lanes(b, 256)].astype(F32)
                both = jnp.concatenate([tot[:8], tot[8:]], axis=1) * scale
                place(12, 2 * b, both[:4])
                place(12, 2 * b + 1, both[4:])
            store(12, 4, 1).start()

    def sent_pieces():
        for p in range(NP):
            ycopy(p).wait_send()
            fcopy(p, c).wait_send()
        for ck in range(2):
            bcopy(ck, c).wait_send()
            for dx in (1, 2, 3):
                xcopy_all(0, ck, dx).wait_send()

    def sent_sums():
        for g in range(2):
            for zi in range(2):
                @pl.when(zbase(g) + zi != z)
                def _(g=g, zi=zi):
                    for nt in range(NB):
                        zcopy(g, nt, zi).wait_send()

            @pl.when(owns(g))
            def _(g=g):
                for nt in range(NB):
                    hcopy(g, nt).wait_send()

        for ck in range(2):
            for dx in (1, 2, 3):
                xcopy_all(1, ck, dx).wait_send()

    def sent_narrow():
        for g in range(2):
            for zi in range(2):
                for hi in range(2):
                    @pl.when(jnp.logical_or(zbase(g) + zi != z, h != hi))
                    def _(g=g, zi=zi, hi=hi):
                        for b in range(2):
                            ncopy(g, b, zi, hi).wait_send()

    advect(0)
    forward(0)
    for ck in range(2):
        bcopy(ck, 1 - c).wait_recv()
    early(0)
    early(1)
    forward(1)
    advect(1)
    forward(2)
    early(2)
    forward(3)
    early(3)
    late_first()
    forward(4)
    late(2, 3)
    late(4)
    forward(5)
    xsum(0, 0, 2)
    late(5, then={1: 6})
    xsum(0, 2, 4)
    forward(7)
    late(6)
    forward(8)
    late(7)
    forward(9)
    xsum_narrow(0)
    late(8, then={1: 10})
    late(9, then={1: 11})
    late(10, then={0: 12, 3: 13})
    late(11)
    xsum(1, 0, 1)
    late(12)
    late(13)
    xsum(1, 1, 4)
    zsum(0)
    zsum(1)
    sent_pieces()
    finish_narrow(0)
    xsum_narrow(1)
    finish(0)
    finish(1)
    sent_sums()
    finish_narrow(1)
    sent_narrow()
    store(0, 12, 0).wait()
    store(12, 4, 1).wait()


def on_device(modes, gradients, convecting_slab, connectivity, weights):
    nodes = modes.shape[2] * lax.axis_size("space")
    scale = (3.0 * nodes) ** (-0.5)
    dma, vmem = pltpu.SemaphoreType.DMA, pltpu.VMEM
    return pl.pallas_call(
        functools.partial(kernel, scale),
        name="convection",
        out_shape=jax.ShapeDtypeStruct((16, 16, 128), F32),
        in_specs=[pl.BlockSpec(memory_space=pl.ANY)] * 5,
        out_specs=pl.BlockSpec(memory_space=pl.ANY),
        scratch_shapes=[
            vmem((3, 128, Q), BF16), vmem((3, 3, 128, Q), BF16), vmem((3, 16, PTS), BF16),
            vmem((1, Q), jnp.int32), vmem((1, Q), F32), vmem((3, 16, Q), F32),
            vmem((3, 256, Q), BF16), vmem((3, 256, Q), BF16),
            vmem((3, 2048, QH), BF16), vmem((3, 2048, QH), BF16), vmem((2048, 192), F32), vmem((2048, 128), F32),
            vmem((2, 4, 48, 2048), BF16), vmem((2, 3, 48, 2048), BF16),
            vmem((2, 4, 16, 2048), BF16), vmem((2, 3, 16, 2048), BF16),
            vmem((2, 2, 16, NB * ZT), BF16), vmem((2, 3, 16, NB * ZT), BF16),
            vmem((2, 2, 16, 2048), F32), vmem((2, 16, 2048), F32),
            vmem((2, 2, 2, 16, 512), BF16), vmem((2, 7, 16, 512), BF16), vmem((16, 16, 128), F32),
            dma((2,)),
            dma((13,)), dma((NP,)), dma((NP,)), dma((NP,)), dma((NP,)), dma((2,)), dma((2,)),
            dma((2, 2, 3)), dma((2, 2, NB, 3)), dma((2, NB, 2)), dma((2, NB, 3)), dma((2, NB)), dma((2, NB)),
            dma((2, 2, 2, 2)), dma((2, 2, 7)),
        ],
        compiler_params=pltpu.CompilerParams(
            collective_id=0, has_side_effects=True, vmem_limit_bytes=60 * 2**20),
        cost_estimate=pl.CostEstimate(flops=2 * 512 * 2048 * 6144, bytes_accessed=7 * 2**20, transcendentals=0),
    )(modes, gradients, convecting_slab, connectivity.reshape(1, Q), weights.reshape(1, Q))


def solution(mesh):
    return jax.shard_map(
        on_device,
        mesh=mesh,
        in_specs=(
            P(None, "mode", "space"),
            P(None, None, "mode", "space"),
            P(None, None, "space"),
            P("space"),
            P("space"),
        ),
        out_specs=P("space", None, "mode"),
        check_vma=False,
    )
```

```python
import functools

import jax
import jax.numpy as jnp
from jax import lax
from jax.experimental import pallas as pl
from jax.experimental.pallas import tpu as pltpu
from jax.sharding import PartitionSpec as P

MESH = pl.DeviceIdType.MESH
F32 = jnp.float32
BF16 = jnp.bfloat16

Q = 2048
QH = 1024
PTS = 1024
NB = 4
NT = 512
ZT = 768
JG = 8

WIDE, NARROW = 0, 1
BEGIN = (0, 192)
DEPTH = (96, 32)
TILES = (24, 8)


PARTS = {ck: [(ck, e, q * QH, QH) for e in range(3) for q in range(2)] for ck in (WIDE, NARROW)}
for part in PARTS.values():
    part[-1:] = [part[-1][:3] + (QH // 2,), part[-1][:2] + (QH + QH // 2, QH // 2)]
PIECES = [PARTS[WIDE][0], PARTS[NARROW][0]] + PARTS[WIDE][1:] + PARTS[NARROW][1:]
NP = len(PIECES)
LAST = (7, 13)
AHEAD = 4


def lanes(nt, width=NT):
    if isinstance(nt, int):
        return pl.ds(nt * width, width)
    return pl.ds(pl.multiple_of(nt * width, width), width)


def first_four(shape):
    return lax.broadcasted_iota(jnp.int32, shape, 0) < 4


def kernel(
    scale,
    modes_hbm, grad_hbm, slab_hbm, conn_hbm, wts_hbm,
    out,
    mod, gr, slab, conn, wts, nod, we, wl, a0, a1, accw, accn,
    sxw, rxw, sxn, rxn, sz, rz, hs, rh, sn, rn, res,
    os, ld, ys, yr, fs, fr, bs, br, xs, xr, zs, zr, hsem, hrem, ns, nr,
):
    s = lax.axis_index("space")
    m = lax.axis_index("mode")
    z, h, x, l, c = s // 8, (s // 4) % 2, s % 4, m // 2, m % 2
    halves = (a0, a1)
    sxs, rxs = (sxw, sxn), (rxw, rxn)

    def dev(z=z, h=h, x=x, l=l, c=c):
        return (z * 8 + h * 4 + x, l * 2 + c)

    def remote(src, dst, send, recv, to):
        return pltpu.make_async_remote_copy(src, dst, send, recv, device_id=to, device_id_type=MESH)

    def core_rows(ck, core):
        return pl.ds(pl.multiple_of(BEGIN[ck] + core * DEPTH[ck], 32), DEPTH[ck])

    def piece(ref, p, core):
        ck, e, at, nodes = PIECES[p]
        return ref.at[e, core_rows(ck, core), pl.ds(at, nodes)]

    def ycopy(p):
        return remote(piece(we, p, c), piece(wl, p, c), ys.at[p], yr.at[p], dev(l=1 - l))

    def fcopy(p, core):
        return remote(piece(wl, p, core), piece(wl, p, core), fs.at[p], fr.at[p], dev(c=1 - c))

    def bcopy(ck, core):
        part = we.at[:, core_rows(ck, core), :]
        return remote(part, part, bs.at[ck], br.at[ck], dev(c=1 - c))

    def xcopy(g, ck, nt, dx):
        to = (x + dx) % 4
        return remote(sxs[ck].at[g, to, :, lanes(nt)], rxs[ck].at[g, dx - 1, :, lanes(nt)],
                      xs.at[g, ck, dx - 1], xr.at[g, ck, nt, dx - 1], dev(x=to))

    def xcopy_all(g, ck, dx):
        to = (x + dx) % 4
        return remote(sxs[ck].at[g, to], rxs[ck].at[g, dx - 1],
                      xs.at[g, ck, dx - 1], xr.at[g, ck, 0, dx - 1], dev(x=to))

    def zbase(g):
        return 2 * l if g == 0 else 2 * (1 - l)

    def owns(g):
        return z // 2 == (l if g == 0 else 1 - l)

    def zcopy(g, nt, zi):
        to = zbase(g) + zi
        slot = (to - z + 3) % 4
        return remote(sz.at[g, zi, :, lanes(nt, ZT)], rz.at[g, slot, :, lanes(nt, ZT)],
                      zs.at[g, nt, zi], zr.at[g, nt, slot], dev(z=to))

    def zrecv(g, nt, slot):
        return remote(sz.at[g, 0, :, lanes(nt, ZT)], rz.at[g, slot, :, lanes(nt, ZT)],
                      zs.at[g, nt, 0], zr.at[g, nt, slot], dev(z=(z + 1) % 4))

    def hcopy(g, nt):
        return remote(hs.at[g, 1 - h, :, lanes(nt)], rh.at[g, :, lanes(nt)],
                      hsem.at[g, nt], hrem.at[g, nt], dev(h=1 - h))

    def ncopy(g, b, zi, hi):
        to = zbase(g) + zi
        slot = ((to - z + 4) % 4) * 2 + (hi - h + 2) % 2 - 1
        return remote(sn.at[g, zi, hi, :, lanes(b, 256)], rn.at[g, slot, :, lanes(b, 256)],
                      ns.at[g, b, zi, hi], nr.at[g, b, slot], dev(z=to, h=hi))

    def nrecv(g, b, slot):
        return remote(sn.at[g, 0, 0, :, lanes(b, 256)], rn.at[g, slot, :, lanes(b, 256)],
                      ns.at[g, b, 0, 0], nr.at[g, b, slot], dev(z=(z + 1) % 4))

    loads = [pltpu.make_async_copy(wts_hbm, wts, ld.at[0])]
    for e in range(3):
        for q in range(2):
            part = (e, slice(None), pl.ds(q * QH, QH))
            loads.append(pltpu.make_async_copy(modes_hbm.at[part], mod.at[part], ld.at[1 + 2 * e + q]))
    loads += [pltpu.make_async_copy(conn_hbm, conn, ld.at[7]), pltpu.make_async_copy(slab_hbm, slab, ld.at[8])]
    for k in range(4):
        part = (slice(None), slice(None), pl.ds(32 * k, 32))
        loads.append(pltpu.make_async_copy(grad_hbm.at[part], gr.at[part], ld.at[9 + k]))
    peers = [dev(c=1 - c), dev(l=1 - l)] + [dev(x=(x + d) % 4) for d in (1, 2, 3)]
    peers += [dev(z=(z + d) % 4, h=(h + k) % 2) for d in range(4) for k in range(2) if d + k > 0]
    for load in loads:
        load.start()
    barrier = pltpu.get_barrier_semaphore()
    for to in peers:
        pl.semaphore_signal(barrier, 1, device_id=to, device_id_type=MESH)

    loads[0].wait()
    for e in range(3):
        def weigh(t, _, e=e):
            ln = lanes(t, 256)
            w = wts[:, ln]
            top = first_four((8, 256))
            wide, narrow = [], []
            for xx in range(4):
                lo = w * mod[e, xx * 16:xx * 16 + 16, ln].astype(F32)
                hi = w * mod[e, 64 + xx * 16:64 + xx * 16 + 16, ln].astype(F32)
                wide += [lo[:8], hi[:8], jnp.where(top, lo[8:], pltpu.roll(hi[8:], 4, 0))]
                narrow.append(jnp.where(top, pltpu.roll(lo[8:], 4, 0), hi[8:]))
            we[e, core_rows(WIDE, c), ln] = jnp.concatenate(wide, axis=0).astype(BF16)
            we[e, core_rows(NARROW, c), ln] = jnp.concatenate(narrow, axis=0).astype(BF16)
            return 0

        for q in range(2):
            loads[1 + 2 * e + q].wait()
            lax.fori_loop(4 * q, 4 * q + 4, weigh, 0)
            if e + q == 0:
                pl.semaphore_wait(barrier, len(peers))
            if e + q == 0:
                ycopy(0).start()
            if 1 + 2 * e + q < AHEAD:
                ycopy(1 + 2 * e + q).start()
    for ck in range(2):
        bcopy(ck, c).start()

    loads[7].wait()
    loads[8].wait()

    def gather(t, _):
        ln = lanes(t)
        local = conn[:, ln] - s * PTS
        hot = (lax.broadcasted_iota(jnp.int32, (128, NT), 0) == local % 128).astype(F32).astype(BF16)
        group = local // 128
        vals = jnp.zeros((48, NT), F32)
        for k in range(PTS // 128):
            one = jnp.dot(slab[:, :, k * 128:(k + 1) * 128].reshape(48, 128), hot, preferred_element_type=F32)
            vals = jnp.where(group == k, one, vals)
        nod[:, :, ln] = vals.reshape(3, 16, NT)
        return 0

    lax.fori_loop(0, NB, gather, 0)

    def forward(p):
        ycopy(p).wait_recv()
        fcopy(p, c).start()
        if p + AHEAD < NP:
            ycopy(p + AHEAD).start()

    def spread(g, ck, nt, tot):
        for xx in range(4):
            both = [tot[k * DEPTH[ck] + xx * TILES[ck]:k * DEPTH[ck] + (xx + 1) * TILES[ck]] for k in range(2)]
            sxs[ck][g, xx, :, lanes(nt)] = jnp.concatenate(both, axis=0).astype(BF16)
        for dx in (1, 2, 3):
            xcopy(g, ck, nt, dx).start()

    def advect(group):
        def some(t, _):
            row = pl.multiple_of((t // 2) * 16, 16)
            at = lanes(t % 2)
            for half in range(2):
                ln = pl.ds(pl.multiple_of(half * QH + (t % 2) * NT, NT), NT)
                for e in range(3):
                    g0, g1, g2 = (gr[d, e, pl.ds(row, 16), ln].astype(F32) for d in range(3))
                    for jj in range(JG):
                        j = group * JG + jj
                        v = nod[0, j:j + 1, ln] * g0 + nod[1, j:j + 1, ln] * g1 + nod[2, j:j + 1, ln] * g2
                        halves[half][e, pl.ds(j * 128 + row, 16), at] = v.astype(BF16)
            return 0

        for k in range(4):
            if group == 0:
                loads[9 + k].wait()
            lax.fori_loop(4 * k, 4 * k + 4, some, 0)

    def early(nt):
        tot = None
        for e in range(3):
            for q in range(2):
                part = lax.dot_general(we[e, :, q * QH:(q + 1) * QH], halves[q][e, nt * NT:(nt + 1) * NT, :],
                                       (((1,), (1,)), ((), ())), preferred_element_type=F32)
                tot = part if tot is None else tot + part
        for ck in range(2):
            spread(0, ck, nt, tot[BEGIN[ck]:BEGIN[ck] + 2 * DEPTH[ck]])

    def product(p, nt, begin, end):
        _, e, at, nodes = PIECES[p]
        a = halves[at // QH][e, nt * NT:(nt + 1) * NT, at % QH:at % QH + nodes]
        return lax.dot_general(a, wl[e, begin:end, at:at + nodes], (((1,), (1,)), ((), ())), preferred_element_type=F32)

    def late_first():
        for p in range(2):
            fcopy(p, 1 - c).wait_recv()
        for nt in range(NB):
            cols = slice(nt * NT, (nt + 1) * NT)
            part = product(0, nt, 0, 256)
            accw[cols, :] = part[:, :192]
            accn[cols, :] = part[:, 128:]

    def late(*ps, then={}):
        ck = PIECES[ps[0]][0]
        for p in ps:
            fcopy(p, 1 - c).wait_recv()
        for nt in range(NB):
            cols = slice(nt * NT, (nt + 1) * NT)
            total = (accw, accn)[ck]
            begin, end = ((0, 192), (128, 256))[ck]
            part = total[cols, :]
            for p in ps:
                part = part + product(p, nt, begin, end)
            if ps[-1] < LAST[ck]:
                total[cols, :] = part
            else:
                rows = part.T
                spread(1, ck, nt, rows if ck == WIDE else rows[64:])
            if nt in then:
                forward(then[nt])

    def xsum(g, begin=0, end=NB):
        def one(nt, _):
            for dx in (1, 2, 3):
                xcopy(g, WIDE, nt, dx).wait_recv()
            tot = sxw[g, x, :, lanes(nt)].astype(F32)
            for i in range(3):
                tot = tot + rxw[g, i, :, lanes(nt)].astype(F32)
            for zi in range(2):
                own = tot[zi * 24:zi * 24 + 24]
                fold = jnp.concatenate([own[16:, :256], own[16:, 256:]], axis=0)
                sz[g, zi, :, lanes(nt, ZT)] = jnp.concatenate([own[:16], fold], axis=1).astype(BF16)

                @pl.when(zbase(g) + zi != z)
                def _(zi=zi):
                    zcopy(g, nt, zi).start()
            return 0

        lax.fori_loop(begin, end, one, 0)

    def zsum(g):
        @pl.when(owns(g))
        def _():
            def one(nt, _):
                for i in range(3):
                    zrecv(g, nt, i).wait_recv()
                tot = sz[g, z % 2, :, lanes(nt, ZT)].astype(F32)
                for i in range(3):
                    tot = tot + rz[g, i, :, lanes(nt, ZT)].astype(F32)
                mixed = jnp.concatenate([tot[:8, NT:], tot[8:, NT:]], axis=1)
                for hi in range(2):
                    pair = jnp.concatenate([tot[hi * 8:hi * 8 + 8, :NT], mixed], axis=0)
                    hs[g, hi, :, lanes(nt)] = pair
                hcopy(g, nt).start()
                return 0

            lax.fori_loop(0, NB, one, 0)

    def place(row, nt, part):
        for jj in range(4):
            res[row:row + part.shape[0], 4 * nt + jj, :] = part[:, jj * 128:(jj + 1) * 128]

    def store(row, rows, k):
        return pltpu.make_async_copy(res.at[pl.ds(row, rows)], out.at[pl.ds(row, rows)], os.at[k])

    def finish(g):
        @pl.when(owns(g))
        def _():
            for nt in range(NB):
                hcopy(g, nt).wait_recv()
                tot = (hs[g, h, :, lanes(nt)].astype(F32) + rh[g, :, lanes(nt)].astype(F32)) * scale
                place(0, nt, tot[:8])
                upper = jnp.where(h == 0, tot[8:], pltpu.roll(tot[8:], 4, 0))
                place(8, nt, upper[:4])
            store(0, 12, 0).start()

    def xsum_narrow(g):
        for b in range(2):
            halved = [[], []]
            for nt in (2 * b, 2 * b + 1):
                for dx in (1, 2, 3):
                    xcopy(g, NARROW, nt, dx).wait_recv()
                tot = sxn[g, x, :, lanes(nt)].astype(F32)
                for i in range(3):
                    tot = tot + rxn[g, i, :, lanes(nt)].astype(F32)
                for zi in range(2):
                    halved[zi].append(tot[zi * 8:zi * 8 + 8])
            top = first_four((8, NT))
            for zi in range(2):
                left, right = halved[zi]
                for hi in range(2):
                    if hi == 0:
                        both = jnp.where(top, left, pltpu.roll(right, 4, 0))
                    else:
                        both = jnp.where(top, pltpu.roll(left, 4, 0), right)
                    fold = jnp.concatenate([both[:, :256], both[:, 256:]], axis=0)
                    sn[g, zi, hi, :, lanes(b, 256)] = fold.astype(BF16)

                    @pl.when(jnp.logical_or(zbase(g) + zi != z, h != hi))
                    def _(zi=zi, hi=hi, b=b):
                        ncopy(g, b, zi, hi).start()

    def finish_narrow(g):
        @pl.when(owns(g))
        def _():
            for b in range(2):
                for i in range(7):
                    nrecv(g, b, i).wait_recv()
                tot = sn[g, z % 2, h, :, lanes(b, 256)].astype(F32)
                for i in range(7):
                    tot = tot + rn[g, i, :, lanes(b, 256)].astype(F32)
                both = jnp.concatenate([tot[:8], tot[8:]], axis=1) * scale
                place(12, 2 * b, both[:4])
                place(12, 2 * b + 1, both[4:])
            store(12, 4, 1).start()

    def sent_pieces():
        for p in range(NP):
            ycopy(p).wait_send()
            fcopy(p, c).wait_send()
        for ck in range(2):
            bcopy(ck, c).wait_send()
            for dx in (1, 2, 3):
                xcopy_all(0, ck, dx).wait_send()

    def sent_sums():
        for g in range(2):
            for zi in range(2):
                @pl.when(zbase(g) + zi != z)
                def _(g=g, zi=zi):
                    for nt in range(NB):
                        zcopy(g, nt, zi).wait_send()

            @pl.when(owns(g))
            def _(g=g):
                for nt in range(NB):
                    hcopy(g, nt).wait_send()

        for ck in range(2):
            for dx in (1, 2, 3):
                xcopy_all(1, ck, dx).wait_send()

    def sent_narrow():
        for g in range(2):
            for zi in range(2):
                for hi in range(2):
                    @pl.when(jnp.logical_or(zbase(g) + zi != z, h != hi))
                    def _(g=g, zi=zi, hi=hi):
                        for b in range(2):
                            ncopy(g, b, zi, hi).wait_send()

    advect(0)
    forward(0)
    for ck in range(2):
        bcopy(ck, 1 - c).wait_recv()
    early(0)
    early(1)
    forward(1)
    advect(1)
    forward(2)
    early(2)
    forward(3)
    early(3)
    late_first()
    forward(4)
    late(2, 3)
    late(4)
    forward(5)
    xsum(0, 0, 2)
    late(5, then={1: 6})
    xsum(0, 2, 4)
    forward(7)
    late(6)
    forward(8)
    late(7)
    forward(9)
    xsum_narrow(0)
    late(8, then={1: 10})
    late(9, then={1: 11})
    late(10, then={0: 12, 3: 13})
    late(11)
    xsum(1, 0, 1)
    late(12)
    late(13)
    xsum(1, 1, 4)
    zsum(0)
    zsum(1)
    sent_pieces()
    finish_narrow(0)
    xsum_narrow(1)
    finish(0)
    finish(1)
    sent_sums()
    finish_narrow(1)
    sent_narrow()
    store(0, 12, 0).wait()
    store(12, 4, 1).wait()


def on_device(modes, gradients, convecting_slab, connectivity, weights):
    nodes = modes.shape[2] * lax.axis_size("space")
    scale = (3.0 * nodes) ** (-0.5)
    dma, vmem = pltpu.SemaphoreType.DMA, pltpu.VMEM
    return pl.pallas_call(
        functools.partial(kernel, scale),
        name="convection",
        out_shape=jax.ShapeDtypeStruct((16, 16, 128), F32),
        in_specs=[pl.BlockSpec(memory_space=pl.ANY)] * 5,
        out_specs=pl.BlockSpec(memory_space=pl.ANY),
        scratch_shapes=[
            vmem((3, 128, Q), BF16), vmem((3, 3, 128, Q), BF16), vmem((3, 16, PTS), BF16),
            vmem((1, Q), jnp.int32), vmem((1, Q), F32), vmem((3, 16, Q), F32),
            vmem((3, 256, Q), BF16), vmem((3, 256, Q), BF16),
            vmem((3, 2048, QH), BF16), vmem((3, 2048, QH), BF16), vmem((2048, 192), F32), vmem((2048, 128), F32),
            vmem((2, 4, 48, 2048), BF16), vmem((2, 3, 48, 2048), BF16),
            vmem((2, 4, 16, 2048), BF16), vmem((2, 3, 16, 2048), BF16),
            vmem((2, 2, 16, NB * ZT), BF16), vmem((2, 3, 16, NB * ZT), BF16),
            vmem((2, 2, 16, 2048), F32), vmem((2, 16, 2048), F32),
            vmem((2, 2, 2, 16, 512), BF16), vmem((2, 7, 16, 512), BF16), vmem((16, 16, 128), F32),
            dma((2,)),
            dma((13,)), dma((NP,)), dma((NP,)), dma((NP,)), dma((NP,)), dma((2,)), dma((2,)),
            dma((2, 2, 3)), dma((2, 2, NB, 3)), dma((2, NB, 2)), dma((2, NB, 3)), dma((2, NB)), dma((2, NB)),
            dma((2, 2, 2, 2)), dma((2, 2, 7)),
        ],
        compiler_params=pltpu.CompilerParams(
            collective_id=0, has_side_effects=True, vmem_limit_bytes=60 * 2**20),
        cost_estimate=pl.CostEstimate(flops=2 * 512 * 2048 * 6144, bytes_accessed=7 * 2**20, transcendentals=0),
    )(modes, gradients, convecting_slab, connectivity.reshape(1, Q), weights.reshape(1, Q))


def solution(mesh):
    return jax.shard_map(
        on_device,
        mesh=mesh,
        in_specs=(
            P(None, "mode", "space"),
            P(None, None, "mode", "space"),
            P(None, None, "space"),
            P("space"),
            P("space"),
        ),
        out_specs=P("space", None, "mode"),
        check_vma=False,
    )
```
